32 devices in a mesh: tri: 32 (over z, y, x, core).
Axes of the slice: x: 2, y: 2, z: 4, core: 2. Of those that a mesh axis runs over, the one named last changes fastest.
Arguments:
- matrix_tiles: bfloat16 [512, 12, 128, 128], P('tri'), may hold values from -0.109375 to 0.109375
- columns: int32 [512, 12], P('tri'), may hold values from 0 to 511, as said below
- vectors: bfloat16 [16, 65536], P(None, 'tri'), may hold values from -6 to 6
- center: float32 [1], replicated, may hold values from -1 to 1
- halfwidth: float32 [1], replicated, may hold values from 1.5 to 3
Outputs:
- filtered_one: float32 [16, 65536], P(None, 'tri')
- filtered_two: float32 [16, 65536], P(None, 'tri')
The draws below stay inside these ranges and needn't reach their ends.
Inputs may be any that keep to these rules, and one draw needn't show every extreme that they name: For block row i, columns[i, k] lies between max(0, (i // 16 - 4) * 16) and i; columns[i, 0] = i and columns[i, 1] = max(0, (i // 16 - 4) * 16); entries may repeat, and repeated tiles add.
All inputs are finite; a program needn't handle non-finite values.
Results may differ from the reference program's by a relative error of at most 0.0018.
Values may be sent and summed in bfloat16 or wider, within the bound.
No kernel may reach another device: no remote copies, remote signals or barrier semaphores. Data moves between devices by JAX's collectives and lax.ppermute only.
A program may use at most 64 MiB of HBM per device.

```python
import jax
import jax.numpy as jnp
from jax import lax

BS = 128
RB = 16
KT = 12
VEC = 16
SPAN = 4
NB = 512
N = 65536


def draw_columns(key, part):
    key = jax.random.fold_in(key, 7)
    row_ids = jnp.arange(NB, dtype=jnp.int32)
    lowest = jnp.maximum(0, (row_ids // RB - SPAN) * RB).astype(jnp.int32)
    picked = jax.random.randint(key, (NB, KT), lowest[:, None], row_ids[:, None] + 1, dtype=jnp.int32)
    picked = picked.at[:, 0].set(row_ids)
    return picked.at[:, 1].set(lowest)


def level_of(rng, shape, split, least, largest):
    def one(dim, blocks):
        steps = jax.random.uniform(jax.random.fold_in(jax.random.fold_in(rng, 6), dim), (blocks,), jnp.float32, least / len(split), largest / len(split))
        return jnp.repeat(jnp.exp(steps), shape[dim] // blocks).reshape((-1,) + (1,) * (len(shape) - dim - 1))

    factor_of = one(*split[0])
    for cut in split[1:]:
        factor_of = factor_of * one(*cut)
    return factor_of


def scatter_about(key, extent, scale, limit, cuts=(), kind=jnp.bfloat16):
    result = scale * jax.random.normal(key, extent, jnp.float32)
    if cuts:
        result = result * level_of(key, extent, cuts, -0.22, 0.18)
    return jnp.clip(result, -limit, limit).astype(kind)


def setup_inputs(seed: int = 0) -> dict:
    keys = jax.random.split(jax.random.key(seed), 6)
    matrix_tiles = scatter_about(keys[0], (NB, KT, BS, BS), (2 * KT * BS) ** -0.5, 0.109375, ((0, 32),))
    columns = draw_columns(jax.random.fold_in(keys[5], 71), 0)
    vectors = scatter_about(keys[2], (VEC, N), 1.0, 6.0, ((1, 32),))
    center = jnp.clip(jax.random.uniform(keys[3], (1,), jnp.float32, -1.0, 1.0), -1.0, 1.0)
    halfwidth = jnp.clip(jax.random.uniform(keys[4], (1,), jnp.float32, 1.5, 3.0), 1.5, 3.0)
    return {"matrix_tiles": matrix_tiles, "columns": columns, "vectors": vectors, "center": center, "halfwidth": halfwidth}


def apply_hamiltonian(matrix_tiles, columns, blocks):
    count_blocks = blocks.shape[0]
    row_ids = jnp.arange(count_blocks, dtype=jnp.int32)
    weight = jnp.where(columns == row_ids[:, None], 0.5, 1.0).astype(jnp.float32)
    groups = count_blocks // RB
    tile_groups = matrix_tiles.reshape(groups, RB, KT, BS, BS)
    column_groups = columns.reshape(groups, RB, KT)
    weight_groups = weight.reshape(groups, RB, KT)
    block_groups = blocks.reshape(groups, RB, VEC, BS)

    def step_group(buffer, items):
        tile_part, column_part, weight_part, own_part = items
        picked = jnp.take(blocks, column_part.reshape(-1), axis=0).reshape(RB, KT, VEC, BS)
        forward = jnp.einsum("rkvc,rkac->rkva", picked.astype(jnp.float32), tile_part.astype(jnp.float32))
        forward = jnp.sum(forward * weight_part[:, :, None, None], axis=1)
        behind = jnp.einsum("rva,rkac->rkvc", own_part.astype(jnp.float32), tile_part.astype(jnp.float32))
        behind = behind * weight_part[:, :, None, None]
        buffer = buffer.at[column_part.reshape(-1)].add(behind.reshape(RB * KT, VEC, BS))
        return buffer, forward

    start = jnp.zeros((count_blocks, VEC, BS), jnp.float32)
    buffer, forward_all = lax.scan(step_group, start, (tile_groups, column_groups, weight_groups, block_groups))
    return forward_all.reshape(count_blocks, VEC, BS) + buffer


def reference(matrix_tiles, columns, vectors, center, halfwidth):
    count_blocks = matrix_tiles.shape[0]
    blocks = vectors.reshape(VEC, count_blocks, BS).transpose(1, 0, 2)
    initial = blocks.astype(jnp.float32)
    product_one = apply_hamiltonian(matrix_tiles, columns, blocks)
    first = (product_one - center[0] * initial) / halfwidth[0]
    rounded = first.astype(jnp.bfloat16)
    product_two = apply_hamiltonian(matrix_tiles, columns, rounded)
    second = 2.0 * (product_two - center[0] * first) / halfwidth[0] - initial
    first_out = first.transpose(1, 0, 2).reshape(VEC, count_blocks * BS)
    second_out = second.transpose(1, 0, 2).reshape(VEC, count_blocks * BS)
    return first_out, second_out
```

```python
import jax
import jax.numpy as jnp
from jax import lax
from jax.experimental import pallas as pl
from jax.experimental.pallas import tpu as pltpu
from jax.sharding import PartitionSpec as P

SPAN = 4
MIB = 1 << 20
LANES = 128


def rotated(block, distance):
    size = lax.axis_size("tri")
    return lax.ppermute(block, "tri", [(i, (i + distance) % size) for i in range(size)])


def exchanged(block):
    return lax.ppermute(block, "tri", [(i, i ^ 1) for i in range(lax.axis_size("tri"))])


def lanes(index, width):
    return pl.ds(pl.multiple_of(index * width, width), width)


def lowest_row(cols):
    return cols[0, 0] - SPAN * cols.shape[0]


def stacked_tiles(tiles, i):
    count = tiles.shape[1]
    return jnp.concatenate(
        [jnp.concatenate([tiles[i + j, k] for k in range(count)], axis=1) for j in range(2)], axis=0
    )


def spread_rows(cols, tiles, own, spread, begin, number):
    rows, count, width, _ = tiles.shape
    vectors = own.shape[0]
    lowest = lowest_row(cols)
    for step in range(0, number, 2):
        i = begin + step
        mine = [own[:, lanes(i + j, width)] for j in range(2)]
        zero = jnp.zeros_like(mine[0])
        both = jnp.concatenate(
            [jnp.concatenate([mine[0], zero], axis=1), jnp.concatenate([zero, mine[1]], axis=1)], axis=0
        )
        product = jnp.dot(both, stacked_tiles(tiles, i), preferred_element_type=jnp.float32)
        for j in range(2):
            for k in range(count):
                column = cols[i + j, k]
                slot = column - lowest
                weight = jnp.where(column == cols[i + j, 0], 0.5, 1.0).astype(jnp.float32)
                place = lanes(lax.rem(slot, rows), width)
                part = product[j * vectors : (j + 1) * vectors, k * width : (k + 1) * width]
                spread[lax.div(slot, rows), :, place] += part * weight


def hand_over(spread, odd, even):
    odd[0] = spread[1]
    odd[1] = spread[3]
    even[0] = spread[0]
    even[1] = spread[2]
    even[2] = spread[4]


def unrolled(rows):
    assert rows % 2 == 0
    return rows if rows <= 16 else 2


def parts_loaded(rows):
    assert rows % 2 == 0
    return [4] * ((rows - 4) // 4) + [2] * ((rows - 4) % 4 // 2) + [2, 2]


def loading_kernel(cols_far, tiles_far, own_far, odd, even, tiles, own, marks, cols, spread, row_sems, sems):
    rows = tiles.shape[0]
    small = [
        pltpu.make_async_copy(cols_far, cols, sems.at[0]),
        pltpu.make_async_copy(own_far, own, sems.at[1]),
    ]
    for copy in small:
        copy.start()
    parts = parts_loaded(rows)

    def part_copy(step):
        some = pl.ds(sum(parts[:step]), parts[step])
        return pltpu.make_async_copy(tiles_far.at[some], tiles.at[some], row_sems.at[step])

    for step in range(len(parts)):
        part_copy(step).start()
    spread[...] = jnp.zeros_like(spread)
    for copy in small:
        copy.wait()
    marks[...] = jnp.full(marks.shape, lax.rem(cols[0, 0] // rows, 2).astype(jnp.float32), jnp.float32)
    for step, number in enumerate(parts):
        part_copy(step).wait()
        spread_rows(cols, tiles, own, spread, sum(parts[:step]), number)
    hand_over(spread, odd, even)


def behind_kernel(cols, tiles, own, odd, even, spread):
    rows = tiles.shape[0]
    spread[...] = jnp.zeros_like(spread)
    together = unrolled(rows)

    def some_rows(step, carry):
        spread_rows(cols, tiles, own, spread, step * together, together)
        return carry

    lax.fori_loop(0, rows // together, some_rows, 0)
    hand_over(spread, odd, even)


def forward_kernel(cols, tiles, own, near, far, other, total, window):
    rows, count, width, _ = tiles.shape
    vectors = own.shape[0]
    window[0] = far[...]
    window[1] = other[1]
    window[2] = near[...]
    window[3] = other[0]
    window[4] = own[...]
    lowest = lowest_row(cols)
    together = unrolled(rows)

    def some_rows(step, carry):
        for start in range(0, together, 2):
            i = step * together + start
            picked = [[], []]
            for j in range(2):
                for k in range(count):
                    column = cols[i + j, k]
                    slot = column - lowest
                    weight = jnp.where(column == cols[i + j, 0], 0.5, 1.0).astype(jnp.bfloat16)
                    block = window[lax.div(slot, rows), :, lanes(lax.rem(slot, rows), width)]
                    picked[j].append(block * weight)
            both = jnp.concatenate([jnp.concatenate(blocks, axis=1) for blocks in picked], axis=0)
            product = lax.dot_general(
                both, stacked_tiles(tiles, i), (((1,), (1,)), ((), ())), preferred_element_type=jnp.float32
            )
            for j in range(2):
                part = product[j * vectors : (j + 1) * vectors, j * width : (j + 1) * width]
                total[:, lanes(i + j, width)] = part
        return carry

    lax.fori_loop(0, rows // together, some_rows, 0)


def cost_of(tiles):
    rows, count, width, _ = tiles.shape
    return pl.CostEstimate(
        flops=2 * rows * count * width * width * 16, bytes_accessed=tiles.size * 2 + MIB, transcendentals=0
    )


SMEM = pl.BlockSpec(memory_space=pltpu.SMEM)
VMEM = pl.BlockSpec(memory_space=pltpu.VMEM)
HBM = pl.BlockSpec(memory_space=pltpu.HBM)


def held(columns, tiles):
    return (
        pltpu.with_memory_space_constraint(columns, pltpu.SMEM),
        pltpu.with_memory_space_constraint(tiles, pltpu.VMEM),
    )


def parts_of(part):
    return jax.ShapeDtypeStruct((2,) + part, jnp.float32), jax.ShapeDtypeStruct((3,) + part, jnp.float32)


def loading(columns, tiles, own):
    part = own.shape
    marks = jax.ShapeDtypeStruct(part, jnp.float32)
    pinned = [pltpu.with_memory_space_constraint(x, pltpu.HBM) for x in (columns, tiles, own)]
    return pl.pallas_call(
        loading_kernel,
        out_shape=parts_of(part) + (pltpu.VMEM(tiles.shape, tiles.dtype), pltpu.VMEM(part, own.dtype), marks, pltpu.SMEM(columns.shape, columns.dtype)),
        in_specs=[HBM] * 3,
        out_specs=(VMEM,) * 5 + (SMEM,),
        scratch_shapes=[
            pltpu.VMEM((SPAN + 1,) + part, jnp.float32),
            pltpu.SemaphoreType.DMA((len(parts_loaded(tiles.shape[0])),)),
            pltpu.SemaphoreType.DMA((2,)),
        ],
        compiler_params=pltpu.CompilerParams(vmem_limit_bytes=24 * MIB),
        cost_estimate=cost_of(tiles),
        name="loading",
    )(*pinned)


def behind(columns, tiles, own):
    part = own.shape
    return pl.pallas_call(
        behind_kernel,
        out_shape=parts_of(part),
        in_specs=[SMEM, VMEM, VMEM],
        out_specs=(VMEM, VMEM),
        scratch_shapes=[pltpu.VMEM((SPAN + 1,) + part, jnp.float32)],
        compiler_params=pltpu.CompilerParams(vmem_limit_bytes=24 * MIB),
        cost_estimate=cost_of(tiles),
        name="behind",
    )(*held(columns, tiles), own)


def forward(columns, tiles, own, near, far, other):
    part = own.shape
    return pl.pallas_call(
        forward_kernel,
        out_shape=jax.ShapeDtypeStruct(part, jnp.float32),
        in_specs=[SMEM] + [VMEM] * 5,
        out_specs=VMEM,
        scratch_shapes=[pltpu.VMEM((SPAN + 1,) + part, own.dtype)],
        compiler_params=pltpu.CompilerParams(vmem_limit_bytes=24 * MIB),
        cost_estimate=cost_of(tiles),
        name="forward",
    )(*held(columns, tiles), own, near, far, other)


def packed(values):
    values = values.astype(jnp.float32)
    largest = jnp.maximum(jnp.max(jnp.abs(values), axis=-1, keepdims=True), 1e-30)
    exponent = jnp.ceil(jnp.log2(largest))
    tail = jnp.broadcast_to(exponent, values.shape[:-1] + (LANES,))
    return jnp.concatenate([values * jnp.exp2(-exponent), tail], axis=-1).astype(jnp.float16)


def unpacked(message):
    width = message.shape[-1] - LANES
    return message[..., :width].astype(jnp.float32) * jnp.exp2(message[..., width : width + 1].astype(jnp.float32))


def per_device(matrix_tiles, columns, vectors, center, halfwidth):
    def fetched(own):
        return rotated(own, 2), rotated(own, 4)

    def applied(own, near, far, odd, even, tiles, second_core, spread_out):
        given = exchanged(odd)
        far, near = lax.optimization_barrier((far, near))
        other = exchanged(jnp.stack([jnp.where(second_core, near, own), jnp.where(second_core, far, near)]))
        kept = even[2] + jnp.where(second_core, 0.0, given[1])
        back = packed(even[:2] + jnp.where(second_core, given, jnp.stack([jnp.zeros_like(kept), given[0]])))
        came_far, came_near = rotated(back[0], -4), rotated(back[1], -2)
        ahead = forward(columns, tiles, own, near, far, other)
        ahead, shift, half = spread_out(ahead)
        ahead, shift, half, came_near, came_far = lax.optimization_barrier((ahead, shift, half, came_near, came_far))
        return ahead + (kept + (unpacked(came_near) + unpacked(came_far))), shift, half

    near, far = fetched(vectors)
    odd, even, tiles, own, marks, columns = loading(columns, matrix_tiles, vectors)
    far, near, odd = lax.optimization_barrier((far, near, odd))
    second_core = marks > 0.5

    def read_scalars(ahead):
        ahead, *scalars = lax.optimization_barrier((ahead, center, halfwidth))
        return (ahead,) + tuple(jnp.broadcast_to(x, ahead.shape) for x in scalars)

    product, centre, half = applied(own, near, far, odd, even, tiles, second_core, read_scalars)
    initial = own.astype(jnp.float32)
    first = (product - centre * initial) / half
    rounded = first.astype(jnp.bfloat16)
    near, far = fetched(rounded)
    odd, even = behind(columns, tiles, rounded)
    product, centre, half = applied(
        rounded, near, far, odd, even, tiles, second_core, lambda ahead: (ahead, centre, half)
    )
    second = 2.0 * (product - centre * first) / half - initial
    return (first, second)


def solution(mesh):
    placed = (P("tri", None, None, None), P("tri", None), P(None, "tri"), P(), P())
    return jax.shard_map(
        per_device,
        mesh=mesh,
        in_specs=placed,
        out_specs=(P(None, "tri"), P(None, "tri")),
        check_vma=False,
    )
```

```python
import jax
import jax.numpy as jnp
from jax import lax
from jax.experimental import pallas as pl
from jax.experimental.pallas import tpu as pltpu
from jax.sharding import PartitionSpec as P

SPAN = 4
MIB = 1 << 20
LANES = 128


def rotated(block, distance):
    size = lax.axis_size("tri")
    return lax.ppermute(block, "tri", [(i, (i + distance) % size) for i in range(size)])


def exchanged(block):
    return lax.ppermute(block, "tri", [(i, i ^ 1) for i in range(lax.axis_size("tri"))])


def lanes(index, width):
    return pl.ds(pl.multiple_of(index * width, width), width)


def lowest_row(cols):
    return cols[0, 0] - SPAN * cols.shape[0]


def stacked_tiles(tiles, i):
    count = tiles.shape[1]
    return jnp.concatenate(
        [jnp.concatenate([tiles[i + j, k] for k in range(count)], axis=1) for j in range(2)], axis=0
    )


def spread_rows(cols, tiles, own, spread, begin, number):
    rows, count, width, _ = tiles.shape
    vectors = own.shape[0]
    lowest = lowest_row(cols)
    for step in range(0, number, 2):
        i = begin + step
        mine = [own[:, lanes(i + j, width)] for j in range(2)]
        zero = jnp.zeros_like(mine[0])
        both = jnp.concatenate(
            [jnp.concatenate([mine[0], zero], axis=1), jnp.concatenate([zero, mine[1]], axis=1)], axis=0
        )
        product = jnp.dot(both, stacked_tiles(tiles, i), preferred_element_type=jnp.float32)
        for j in range(2):
            for k in range(count):
                column = cols[i + j, k]
                slot = column - lowest
                weight = jnp.where(column == cols[i + j, 0], 0.5, 1.0).astype(jnp.float32)
                place = lanes(lax.rem(slot, rows), width)
                part = product[j * vectors : (j + 1) * vectors, k * width : (k + 1) * width]
                spread[lax.div(slot, rows), :, place] += part * weight


def hand_over(spread, odd, even):
    odd[0] = spread[1]
    odd[1] = spread[3]
    even[0] = spread[0]
    even[1] = spread[2]
    even[2] = spread[4]


def unrolled(rows):
    assert rows % 2 == 0
    return rows if rows <= 16 else 2


def parts_loaded(rows):
    assert rows % 2 == 0
    return [4] * ((rows - 4) // 4) + [2] * ((rows - 4) % 4 // 2) + [2, 2]


def loading_kernel(cols_far, tiles_far, own_far, odd, even, tiles, own, marks, cols, spread, row_sems, sems):
    rows = tiles.shape[0]
    small = [
        pltpu.make_async_copy(cols_far, cols, sems.at[0]),
        pltpu.make_async_copy(own_far, own, sems.at[1]),
    ]
    for copy in small:
        copy.start()
    parts = parts_loaded(rows)

    def part_copy(step):
        some = pl.ds(sum(parts[:step]), parts[step])
        return pltpu.make_async_copy(tiles_far.at[some], tiles.at[some], row_sems.at[step])

    for step in range(len(parts)):
        part_copy(step).start()
    spread[...] = jnp.zeros_like(spread)
    for copy in small:
        copy.wait()
    marks[...] = jnp.full(marks.shape, lax.rem(cols[0, 0] // rows, 2).astype(jnp.float32), jnp.float32)
    for step, number in enumerate(parts):
        @pl.when(cols[0, 0] >= 0)
        def _():
            part_copy(step).wait()
            spread_rows(cols, tiles, own, spread, sum(parts[:step]), number)

    hand_over(spread, odd, even)


def behind_kernel(cols, tiles, own, odd, even, spread):
    rows = tiles.shape[0]
    spread[...] = jnp.zeros_like(spread)
    together = unrolled(rows)

    def some_rows(step, carry):
        spread_rows(cols, tiles, own, spread, step * together, together)
        return carry

    lax.fori_loop(0, rows // together, some_rows, 0)
    hand_over(spread, odd, even)


def forward_kernel(cols, tiles, own, near, far, other, total, window):
    rows, count, width, _ = tiles.shape
    vectors = own.shape[0]
    window[0] = far[...]
    window[1] = other[1]
    window[2] = near[...]
    window[3] = other[0]
    window[4] = own[...]
    lowest = lowest_row(cols)
    together = unrolled(rows)

    def some_rows(step, carry):
        for start in range(0, together, 2):
            i = step * together + start
            picked = [[], []]
            for j in range(2):
                for k in range(count):
                    column = cols[i + j, k]
                    slot = column - lowest
                    weight = jnp.where(column == cols[i + j, 0], 0.5, 1.0).astype(jnp.bfloat16)
                    block = window[lax.div(slot, rows), :, lanes(lax.rem(slot, rows), width)]
                    picked[j].append(block * weight)
            both = jnp.concatenate([jnp.concatenate(blocks, axis=1) for blocks in picked], axis=0)
            product = lax.dot_general(
                both, stacked_tiles(tiles, i), (((1,), (1,)), ((), ())), preferred_element_type=jnp.float32
            )
            for j in range(2):
                part = product[j * vectors : (j + 1) * vectors, j * width : (j + 1) * width]
                total[:, lanes(i + j, width)] = part
        return carry

    lax.fori_loop(0, rows // together, some_rows, 0)


def cost_of(tiles):
    rows, count, width, _ = tiles.shape
    return pl.CostEstimate(
        flops=2 * rows * count * width * width * 16, bytes_accessed=tiles.size * 2 + MIB, transcendentals=0
    )


SMEM = pl.BlockSpec(memory_space=pltpu.SMEM)
VMEM = pl.BlockSpec(memory_space=pltpu.VMEM)
HBM = pl.BlockSpec(memory_space=pltpu.HBM)


def held(columns, tiles):
    return (
        pltpu.with_memory_space_constraint(columns, pltpu.SMEM),
        pltpu.with_memory_space_constraint(tiles, pltpu.VMEM),
    )


def parts_of(part):
    return jax.ShapeDtypeStruct((2,) + part, jnp.float32), jax.ShapeDtypeStruct((3,) + part, jnp.float32)


def loading(columns, tiles, own):
    part = own.shape
    marks = jax.ShapeDtypeStruct(part, jnp.float32)
    pinned = [pltpu.with_memory_space_constraint(x, pltpu.HBM) for x in (columns, tiles, own)]
    return pl.pallas_call(
        loading_kernel,
        out_shape=parts_of(part) + (pltpu.VMEM(tiles.shape, tiles.dtype), pltpu.VMEM(part, own.dtype), marks, pltpu.SMEM(columns.shape, columns.dtype)),
        in_specs=[HBM] * 3,
        out_specs=(VMEM,) * 5 + (SMEM,),
        scratch_shapes=[
            pltpu.VMEM((SPAN + 1,) + part, jnp.float32),
            pltpu.SemaphoreType.DMA((len(parts_loaded(tiles.shape[0])),)),
            pltpu.SemaphoreType.DMA((2,)),
        ],
        compiler_params=pltpu.CompilerParams(vmem_limit_bytes=24 * MIB),
        cost_estimate=cost_of(tiles),
        name="loading",
    )(*pinned)


def behind(columns, tiles, own):
    part = own.shape
    return pl.pallas_call(
        behind_kernel,
        out_shape=parts_of(part),
        in_specs=[SMEM, VMEM, VMEM],
        out_specs=(VMEM, VMEM),
        scratch_shapes=[pltpu.VMEM((SPAN + 1,) + part, jnp.float32)],
        compiler_params=pltpu.CompilerParams(vmem_limit_bytes=24 * MIB),
        cost_estimate=cost_of(tiles),
        name="behind",
    )(*held(columns, tiles), own)


def forward(columns, tiles, own, near, far, other):
    part = own.shape
    return pl.pallas_call(
        forward_kernel,
        out_shape=jax.ShapeDtypeStruct(part, jnp.float32),
        in_specs=[SMEM] + [VMEM] * 5,
        out_specs=VMEM,
        scratch_shapes=[pltpu.VMEM((SPAN + 1,) + part, own.dtype)],
        compiler_params=pltpu.CompilerParams(vmem_limit_bytes=24 * MIB),
        cost_estimate=cost_of(tiles),
        name="forward",
    )(*held(columns, tiles), own, near, far, other)


def packed(values):
    values = values.astype(jnp.float32)
    largest = jnp.maximum(jnp.max(jnp.abs(values), axis=-1, keepdims=True), 1e-30)
    exponent = jnp.ceil(jnp.log2(largest))
    tail = jnp.broadcast_to(exponent, values.shape[:-1] + (LANES,))
    return jnp.concatenate([values * jnp.exp2(-exponent), tail], axis=-1).astype(jnp.float16)


def unpacked(message):
    width = message.shape[-1] - LANES
    return message[..., :width].astype(jnp.float32) * jnp.exp2(message[..., width : width + 1].astype(jnp.float32))


def per_device(matrix_tiles, columns, vectors, center, halfwidth):
    def fetched(own):
        return rotated(own, 2), rotated(own, 4)

    def applied(own, near, far, odd, even, tiles, second_core, spread_out):
        given = exchanged(odd)
        far, near = lax.optimization_barrier((far, near))
        other = exchanged(jnp.stack([jnp.where(second_core, near, own), jnp.where(second_core, far, near)]))
        kept = even[2] + jnp.where(second_core, 0.0, given[1])
        back = packed(even[:2] + jnp.where(second_core, given, jnp.stack([jnp.zeros_like(kept), given[0]])))
        came_far, came_near = rotated(back[0], -4), rotated(back[1], -2)
        ahead = forward(columns, tiles, own, near, far, other)
        ahead, shift, half = spread_out(ahead)
        ahead, shift, half, came_near, came_far = lax.optimization_barrier((ahead, shift, half, came_near, came_far))
        return ahead + (kept + (unpacked(came_near) + unpacked(came_far))), shift, half

    near, far = fetched(vectors)
    odd, even, tiles, own, marks, columns = loading(columns, matrix_tiles, vectors)
    far, near, odd = lax.optimization_barrier((far, near, odd))
    second_core = marks > 0.5

    def read_scalars(ahead):
        ahead, *scalars = lax.optimization_barrier((ahead, center, halfwidth))
        return (ahead,) + tuple(jnp.broadcast_to(x, ahead.shape) for x in scalars)

    product, centre, half = applied(own, near, far, odd, even, tiles, second_core, read_scalars)
    initial = own.astype(jnp.float32)
    first = (product - centre * initial) / half
    rounded = first.astype(jnp.bfloat16)
    near, far = fetched(rounded)
    odd, even = behind(columns, tiles, rounded)
    product, centre, half = applied(
        rounded, near, far, odd, even, tiles, second_core, lambda ahead: (ahead, centre, half)
    )
    second = 2.0 * (product - centre * first) / half - initial
    return (first, second)


def solution(mesh):
    placed = (P("tri", None, None, None), P("tri", None), P(None, "tri"), P(), P())
    return jax.shard_map(
        per_device,
        mesh=mesh,
        in_specs=placed,
        out_specs=(P(None, "tri"), P(None, "tri")),
        check_vma=False,
    )
```

```python
import jax
import jax.numpy as jnp
from jax import lax
from jax.experimental import pallas as pl
from jax.experimental.pallas import tpu as pltpu
from jax.sharding import PartitionSpec as P

SPAN = 4
MIB = 1 << 20
LANES = 128


def rotated(block, distance):
    size = lax.axis_size("tri")
    return lax.ppermute(block, "tri", [(i, (i + distance) % size) for i in range(size)])


def exchanged(block):
    return lax.ppermute(block, "tri", [(i, i ^ 1) for i in range(lax.axis_size("tri"))])


def lanes(index, width):
    return pl.ds(pl.multiple_of(index * width, width), width)


def lowest_row(cols):
    return cols[0, 0] - SPAN * cols.shape[0]


def stacked_tiles(tiles, i):
    count = tiles.shape[1]
    return jnp.concatenate(
        [jnp.concatenate([tiles[i + j, k] for k in range(count)], axis=1) for j in range(2)], axis=0
    )


def spread_rows(cols, tiles, own, spread, begin, number):
    rows, count, width, _ = tiles.shape
    vectors = own.shape[0]
    lowest = lowest_row(cols)
    for step in range(0, number, 2):
        i = begin + step
        mine = [own[:, lanes(i + j, width)] for j in range(2)]
        zero = jnp.zeros_like(mine[0])
        both = jnp.concatenate(
            [jnp.concatenate([mine[0], zero], axis=1), jnp.concatenate([zero, mine[1]], axis=1)], axis=0
        )
        product = jnp.dot(both, stacked_tiles(tiles, i), preferred_element_type=jnp.float32)
        for j in range(2):
            for k in range(count):
                column = cols[i + j, k]
                slot = column - lowest
                weight = jnp.where(column == cols[i + j, 0], 0.5, 1.0).astype(jnp.float32)
                place = lanes(lax.rem(slot, rows), width)
                part = product[j * vectors : (j + 1) * vectors, k * width : (k + 1) * width]
                spread[lax.div(slot, rows), :, place] += part * weight


def hand_over(spread, odd, even):
    odd[0] = spread[1]
    odd[1] = spread[3]
    even[0] = spread[0]
    even[1] = spread[2]
    even[2] = spread[4]


def unrolled(rows):
    assert rows % 2 == 0
    return rows if rows <= 16 else 2


def parts_loaded(rows):
    assert rows % 2 == 0
    return [4] * ((rows - 4) // 4) + [2] * ((rows - 4) % 4 // 2) + [2, 2]


def loading_kernel(cols_far, tiles_far, own_far, odd, even, tiles, own, marks, cols, spread, row_sems, sems):
    rows = tiles.shape[0]
    small = [
        pltpu.make_async_copy(cols_far, cols, sems.at[0]),
        pltpu.make_async_copy(own_far, own, sems.at[1]),
    ]
    for copy in small:
        copy.start()
    parts = parts_loaded(rows)

    def part_copy(step):
        some = pl.ds(sum(parts[:step]), parts[step])
        return pltpu.make_async_copy(tiles_far.at[some], tiles.at[some], row_sems.at[step])

    for step in range(len(parts)):
        part_copy(step).start()
    spread[...] = jnp.zeros_like(spread)
    for copy in small:
        copy.wait()
    marks[...] = jnp.full(marks.shape, lax.rem(cols[0, 0] // rows, 2).astype(jnp.float32), jnp.float32)
    for step, number in enumerate(parts):
        @pl.when(cols[0, 0] >= 0)
        def _():
            part_copy(step).wait()
            spread_rows(cols, tiles, own, spread, sum(parts[:step]), number)

    hand_over(spread, odd, even)


def behind_kernel(cols, tiles, own, odd, even, spread):
    rows = tiles.shape[0]
    spread[...] = jnp.zeros_like(spread)
    together = unrolled(rows)

    def some_rows(step, carry):
        spread_rows(cols, tiles, own, spread, step * together, together)
        return carry

    lax.fori_loop(0, rows // together, some_rows, 0)
    hand_over(spread, odd, even)


def forward_kernel(cols, tiles, own, near, far, other, total, window):
    rows, count, width, _ = tiles.shape
    vectors = own.shape[0]
    window[0] = far[...]
    window[1] = other[1]
    window[2] = near[...]
    window[3] = other[0]
    window[4] = own[...]
    lowest = lowest_row(cols)
    together = unrolled(rows)

    def some_rows(step, carry):
        for start in range(0, together, 2):
            i = step * together + start
            picked = [[], []]
            for j in range(2):
                for k in range(count):
                    column = cols[i + j, k]
                    slot = column - lowest
                    weight = jnp.where(column == cols[i + j, 0], 0.5, 1.0).astype(jnp.bfloat16)
                    block = window[lax.div(slot, rows), :, lanes(lax.rem(slot, rows), width)]
                    picked[j].append(block * weight)
            both = jnp.concatenate([jnp.concatenate(blocks, axis=1) for blocks in picked], axis=0)
            product = lax.dot_general(
                both, stacked_tiles(tiles, i), (((1,), (1,)), ((), ())), preferred_element_type=jnp.float32
            )
            for j in range(2):
                part = product[j * vectors : (j + 1) * vectors, j * width : (j + 1) * width]
                total[:, lanes(i + j, width)] = part
        return carry

    lax.fori_loop(0, rows // together, some_rows, 0)


def cost_of(tiles):
    rows, count, width, _ = tiles.shape
    return pl.CostEstimate(
        flops=2 * rows * count * width * width * 16, bytes_accessed=tiles.size * 2 + MIB, transcendentals=0
    )


SMEM = pl.BlockSpec(memory_space=pltpu.SMEM)
VMEM = pl.BlockSpec(memory_space=pltpu.VMEM)
HBM = pl.BlockSpec(memory_space=pltpu.HBM)


def held(columns, tiles):
    return (
        pltpu.with_memory_space_constraint(columns, pltpu.SMEM),
        pltpu.with_memory_space_constraint(tiles, pltpu.VMEM),
    )


def parts_of(part):
    return jax.ShapeDtypeStruct((2,) + part, jnp.float32), jax.ShapeDtypeStruct((3,) + part, jnp.float32)


def loading(columns, tiles, own):
    part = own.shape
    marks = jax.ShapeDtypeStruct(part, jnp.float32)
    pinned = [pltpu.with_memory_space_constraint(x, pltpu.HBM) for x in (columns, tiles, own)]
    return pl.pallas_call(
        loading_kernel,
        out_shape=parts_of(part) + (pltpu.VMEM(tiles.shape, tiles.dtype), pltpu.VMEM(part, own.dtype), marks, pltpu.SMEM(columns.shape, columns.dtype)),
        in_specs=[HBM] * 3,
        out_specs=(VMEM,) * 5 + (SMEM,),
        scratch_shapes=[
            pltpu.VMEM((SPAN + 1,) + part, jnp.float32),
            pltpu.SemaphoreType.DMA((len(parts_loaded(tiles.shape[0])),)),
            pltpu.SemaphoreType.DMA((2,)),
        ],
        compiler_params=pltpu.CompilerParams(vmem_limit_bytes=24 * MIB),
        cost_estimate=cost_of(tiles),
        name="loading",
    )(*pinned)


def behind(columns, tiles, own):
    part = own.shape
    return pl.pallas_call(
        behind_kernel,
        out_shape=parts_of(part),
        in_specs=[SMEM, VMEM, VMEM],
        out_specs=(VMEM, VMEM),
        scratch_shapes=[pltpu.VMEM((SPAN + 1,) + part, jnp.float32)],
        compiler_params=pltpu.CompilerParams(vmem_limit_bytes=24 * MIB),
        cost_estimate=cost_of(tiles),
        name="behind",
    )(*held(columns, tiles), own)


def forward(columns, tiles, own, near, far, other):
    part = own.shape
    return pl.pallas_call(
        forward_kernel,
        out_shape=jax.ShapeDtypeStruct(part, jnp.float32),
        in_specs=[SMEM] + [VMEM] * 5,
        out_specs=VMEM,
        scratch_shapes=[pltpu.VMEM((SPAN + 1,) + part, own.dtype)],
        compiler_params=pltpu.CompilerParams(vmem_limit_bytes=24 * MIB),
        cost_estimate=cost_of(tiles),
        name="forward",
    )(*held(columns, tiles), own, near, far, other)


def packed(values):
    values = values.astype(jnp.float32)
    largest = jnp.maximum(jnp.max(jnp.abs(values), axis=-1, keepdims=True), 1e-30)
    exponent = jnp.ceil(jnp.log2(largest))
    tail = jnp.broadcast_to(exponent, values.shape[:-1] + (LANES,))
    return jnp.concatenate([values * jnp.exp2(-exponent), tail], axis=-1).astype(jnp.float16)


def unpacked(message):
    width = message.shape[-1] - LANES
    return message[..., :width].astype(jnp.float32) * jnp.exp2(message[..., width : width + 1].astype(jnp.float32))


def rounded_to_send(values):
    return values.astype(jnp.bfloat16)


def widened(message):
    return message.astype(jnp.float32)


def per_device(matrix_tiles, columns, vectors, center, halfwidth):
    def fetched(own):
        return rotated(own, 2), rotated(own, 4)

    def applied(own, near, far, odd, even, tiles, second_core, spread_out, pack, unpack):
        given = exchanged(odd)
        far, near = lax.optimization_barrier((far, near))
        other = exchanged(jnp.stack([jnp.where(second_core, near, own), jnp.where(second_core, far, near)]))
        kept = even[2] + jnp.where(second_core, 0.0, given[1])
        back = pack(even[:2] + jnp.where(second_core, given, jnp.stack([jnp.zeros_like(kept), given[0]])))
        came_far, came_near = rotated(back[0], -4), rotated(back[1], -2)
        ahead = forward(columns, tiles, own, near, far, other)
        ahead, shift, half = spread_out(ahead)
        ahead, shift, half, came_near, came_far = lax.optimization_barrier((ahead, shift, half, came_near, came_far))
        return ahead + (kept + (unpack(came_near) + unpack(came_far))), shift, half

    near, far = fetched(vectors)
    odd, even, tiles, own, marks, columns = loading(columns, matrix_tiles, vectors)
    far, near, odd = lax.optimization_barrier((far, near, odd))
    second_core = marks > 0.5

    def read_scalars(ahead):
        ahead, *scalars = lax.optimization_barrier((ahead, center, halfwidth))
        return (ahead,) + tuple(jnp.broadcast_to(x, ahead.shape) for x in scalars)

    product, centre, half = applied(own, near, far, odd, even, tiles, second_core, read_scalars, packed, unpacked)
    initial = own.astype(jnp.float32)
    first = (product - centre * initial) / half
    rounded = first.astype(jnp.bfloat16)
    near, far = fetched(rounded)
    odd, even = behind(columns, tiles, rounded)
    product, centre, half = applied(
        rounded, near, far, odd, even, tiles, second_core, lambda ahead: (ahead, centre, half), rounded_to_send, widened
    )
    second = 2.0 * (product - centre * first) / half - initial
    return (first, second)


def solution(mesh):
    placed = (P("tri", None, None, None), P("tri", None), P(None, "tri"), P(), P())
    return jax.shard_map(
        per_device,
        mesh=mesh,
        in_specs=placed,
        out_specs=(P(None, "tri"), P(None, "tri")),
        check_vma=False,
    )
```
